512 devices in a mesh: wide: 64 (over z, y), narrow: 8 (over x, core).
Axes of the slice: x: 4, y: 4, z: 16, core: 2. Of those that a mesh axis runs over, the one named last changes fastest.
Arguments:
- gathered_rows: bfloat16 [64, 512, 128], P('wide', 'narrow'), may hold values from -0.59765625 to 0.59765625
- bag_counts: int32 [64, 512, 10240], P('wide', 'narrow'), may hold values from 0 to 2, as said below
- row_state: float32 [64, 512], P('wide', 'narrow'), may hold values from 100 to 10000
- cross_down: bfloat16 [512, 8192], P('narrow'), may hold values from -0.0625 to 0.0625
- cross_up: bfloat16 [512, 8192], P('narrow'), may hold values from -0.25 to 0.25
- cross_bias: float32 [8192], replicated, may hold values from -3 to 3
- upstream: bfloat16 [10240, 8192], P('wide', 'narrow'), may hold values from -6 to 6
Outputs:
- crossed: bfloat16 [10240, 8192], P('wide', 'narrow')
- new_rows: float32 [64, 512, 128], P('wide', 'narrow')
The draws below stay inside these ranges and needn't reach their ends.
Inputs may be any that keep to these rules, and one draw needn't show every extreme that they name: `bag_counts`: each sample's bag holds each gathered row at most twice; most entries are zero.
All inputs are finite; a program needn't handle non-finite values.
Results may differ from the reference program's by a relative error of at most 0.028.
Values may be sent and summed in bfloat16 or wider, within the bound.
A program may use at most 64 MiB of HBM per device.

```python
import math
import jax
import jax.numpy as jnp
from jax import lax

E = 128
RANK = 512
ROWS_DEV = 64
TABLES = 64
SLOTS = 512
BATCH = 10240
FEAT = 8192
N_NARROW = 8


def draw_bag_counts(key, part):
    key = jax.random.fold_in(key, 11)
    raw_draw = jax.random.randint(key, (TABLES, SLOTS, BATCH), 0, 32)
    ones_part = (raw_draw < 2).astype(jnp.int32)
    twos_part = (raw_draw == 2).astype(jnp.int32) * 2
    return (ones_part + twos_part).astype(jnp.int32)


def block_levels(key, shape, pieces, low, largest):
    loudness, own = 1.0, jax.random.fold_in(key, 6)
    for dim, parts in pieces:
        heights = jnp.exp(jax.random.uniform(jax.random.fold_in(own, dim), (parts,), jnp.float32, low / len(pieces), largest / len(pieces)))
        loudness = loudness * jnp.repeat(heights, shape[dim] // parts).reshape([-1 if axis == dim else 1 for axis in range(len(shape))])
    return loudness


def centred(key, shape, spread, limit, shards=(), kind=jnp.bfloat16):
    entries = spread * jax.random.normal(key, shape, jnp.float32)
    if shards:
        entries = entries * block_levels(key, shape, shards, -0.22, 0.18)
    return jnp.clip(entries, -limit, limit).astype(kind)


def setup_inputs(seed: int = 0) -> dict:
    arg_keys = jax.random.split(jax.random.key(seed), 8)
    gathered_rows = centred(arg_keys[0], (TABLES, SLOTS, E), 0.1, 0.59765625, ((0, 64), (1, 8)))
    bag_counts = draw_bag_counts(jax.random.fold_in(arg_keys[7], 71), 0)
    row_state = jnp.clip(jnp.exp(math.log(10000.0) - 4.6051702 * jax.random.uniform(arg_keys[2], (TABLES, SLOTS), jnp.float32) ** block_levels(arg_keys[2], (TABLES, SLOTS), ((0, 64), (1, 8)), -0.2, 0.2)), 100.0, 10000.0)
    cross_down = centred(arg_keys[3], (RANK, FEAT), FEAT ** -0.5, 0.0625, ((0, 8),))
    cross_up = centred(arg_keys[4], (RANK, FEAT), RANK ** -0.5, 0.25, ((0, 8),))
    cross_bias = centred(arg_keys[5], (FEAT,), 0.5, 3.0, (), jnp.float32)
    upstream = centred(arg_keys[6], (BATCH, FEAT), 1.0, 6.0, ((0, 64), (1, 8)))
    return {"gathered_rows": gathered_rows, "bag_counts": bag_counts, "row_state": row_state, "cross_down": cross_down, "cross_up": cross_up, "cross_bias": cross_bias, "upstream": upstream}


learning_rate = 0.2

def pool_table(pair):
    table_rows, table_counts = pair
    rows_blocks = table_rows.reshape(N_NARROW, ROWS_DEV, E).astype(jnp.float32)
    count_blocks = table_counts.reshape(N_NARROW, ROWS_DEV, BATCH).astype(jnp.float32)
    partial_value = jnp.einsum('srb,sre->sbe', count_blocks, rows_blocks)
    partial_value = lax.optimization_barrier(partial_value.astype(jnp.bfloat16)).astype(jnp.float32)
    return lax.optimization_barrier(jnp.sum(partial_value, axis=0)).astype(jnp.bfloat16)

def table_grad(pair):
    table_counts, column_grad = pair
    return jnp.dot(table_counts.astype(jnp.bfloat16), column_grad, preferred_element_type=jnp.float32)

def reference(gathered_rows, bag_counts, row_state, cross_down, cross_up, cross_bias, upstream):
    pooled = lax.map(pool_table, (gathered_rows, bag_counts))
    dense_in = pooled.transpose(1, 0, 2).reshape(BATCH, FEAT)
    block = RANK // N_NARROW
    low = jnp.dot(dense_in, cross_down.T, preferred_element_type=jnp.float32).astype(jnp.bfloat16)
    lifted = jnp.zeros((BATCH, FEAT), jnp.float32)
    for block_index in range(N_NARROW):
        piece = jnp.dot(low[:, block_index * block:(block_index + 1) * block], cross_up[block_index * block:(block_index + 1) * block], preferred_element_type=jnp.float32)
        lifted = lifted + lax.optimization_barrier(piece.astype(jnp.bfloat16)).astype(jnp.float32)
    dense_full = dense_in.astype(jnp.float32)
    crossed = (dense_full * (lifted + cross_bias) + dense_full).astype(jnp.bfloat16)
    grad_out = upstream.astype(jnp.float32)
    scaled = (grad_out * dense_full).astype(jnp.bfloat16)
    rank_grad = jnp.dot(scaled, cross_up.T, preferred_element_type=jnp.float32).astype(jnp.bfloat16)
    back_total = jnp.zeros((BATCH, FEAT), jnp.float32)
    for block_index in range(N_NARROW):
        piece = jnp.dot(rank_grad[:, block_index * block:(block_index + 1) * block], cross_down[block_index * block:(block_index + 1) * block], preferred_element_type=jnp.float32)
        back_total = back_total + lax.optimization_barrier(piece.astype(jnp.bfloat16)).astype(jnp.float32)
    input_grad = (grad_out * (lifted + cross_bias + 1.0) + back_total).astype(jnp.bfloat16)
    per_table = input_grad.reshape(BATCH, TABLES, E).transpose(1, 0, 2)
    row_grad = lax.map(table_grad, (bag_counts, per_table))
    state = row_state + lax.optimization_barrier(jnp.mean(row_grad * row_grad, axis=-1))
    new_rows = gathered_rows.astype(jnp.float32) - learning_rate * row_grad / jnp.sqrt(state)[..., None]
    return (crossed, new_rows)
```

```python
import jax
import jax.numpy as jnp
from jax import lax
from jax.sharding import PartitionSpec as P

learning_rate = 0.2


def on_device(gathered_rows, bag_counts, row_state, cross_down, cross_up, cross_bias, upstream):
    f32, bf16 = jnp.float32, jnp.bfloat16
    n = lax.axis_size("narrow")
    wide = lax.axis_size("wide")
    rows_dev, emb = gathered_rows.shape[1:]
    batch = bag_counts.shape[2]
    block, cols = upstream.shape
    sub = block // n
    counts = bag_counts[0].astype(bf16).reshape(rows_dev, wide, n, sub).transpose(2, 0, 1, 3)
    counts = lax.all_to_all(
        counts.reshape(n, rows_dev, wide * sub), "narrow", split_axis=0, concat_axis=0, tiled=True
    ).reshape(n * rows_dev, wide * sub)
    rows_all = lax.all_gather(gathered_rows[0], "narrow", axis=0, tiled=True)
    rank_dev = cross_down.shape[0]
    both = jnp.stack([cross_down, cross_up]).reshape(2 * rank_dev, n, cols).transpose(1, 0, 2)
    both = lax.all_to_all(both, "narrow", split_axis=0, concat_axis=0, tiled=True)
    down = both[:, :rank_dev].reshape(n * rank_dev, cols)
    up = both[:, rank_dev:].reshape(n * rank_dev, cols)

    pooled = lax.dot_general(
        counts, rows_all, (((0,), (0,)), ((), ())), preferred_element_type=f32
    ).astype(bf16)
    pooled = lax.all_to_all(
        pooled.reshape(wide, sub, emb), "wide", split_axis=0, concat_axis=0, tiled=True
    )
    dense = lax.all_to_all(pooled, "narrow", split_axis=0, concat_axis=0, tiled=True)
    dense = dense.reshape(n, wide // n, sub, emb).transpose(0, 2, 1, 3).reshape(block, cols)
    dense_f = dense.astype(f32)
    grad_f = upstream.astype(f32)
    scaled = (grad_f * dense_f).astype(bf16)
    contract_cols = (((1,), (1,)), ((), ()))
    low = lax.dot_general(dense, down, contract_cols, preferred_element_type=f32)
    rank_grad = lax.dot_general(scaled, up, contract_cols, preferred_element_type=f32)
    ranks = lax.psum(jnp.concatenate([low, rank_grad], axis=1).astype(bf16), "narrow")
    low, rank_grad = jnp.split(ranks, 2, axis=1)
    lifted = jnp.dot(low, up, preferred_element_type=f32)
    back = jnp.dot(rank_grad, down, preferred_element_type=f32)
    bias = lax.dynamic_slice_in_dim(cross_bias, lax.axis_index("narrow") * cols, cols, 0)
    crossed = (dense_f * (lifted + bias) + dense_f).astype(bf16)
    grad = (grad_f * (lifted + bias + 1.0) + back).astype(bf16)
    grad = grad.reshape(n, sub, wide // n, emb).transpose(0, 2, 1, 3)
    grad = lax.all_to_all(grad, "narrow", split_axis=0, concat_axis=0, tiled=True)
    grad = lax.all_to_all(
        grad.reshape(wide, sub, emb), "wide", split_axis=0, concat_axis=0, tiled=True
    ).reshape(wide * sub, emb)
    row_grad = jnp.dot(counts, grad, preferred_element_type=f32)
    row_grad = lax.psum_scatter(row_grad, "narrow", scatter_dimension=0, tiled=True)
    state = row_state[0] + jnp.mean(row_grad * row_grad, axis=1)
    new_rows = (
        gathered_rows[0].astype(f32) - learning_rate * row_grad / jnp.sqrt(state)[:, None]
    )
    return (crossed, new_rows[None])


def solution(mesh):
    placed = (
        P("wide", "narrow", None),
        P("wide", "narrow", None),
        P("wide", "narrow"),
        P("narrow", None),
        P("narrow", None),
        P(),
        P("wide", "narrow"),
    )
    return jax.shard_map(
        on_device,
        mesh=mesh,
        in_specs=placed,
        out_specs=(P("wide", "narrow"), P("wide", "narrow", None)),
        check_vma=False,
    )
```

```python
import functools
import jax
import jax.numpy as jnp
from jax import lax
from jax.experimental import pallas as pl
from jax.experimental.pallas import tpu as pltpu
from jax.sharding import PartitionSpec as P

learning_rate = 0.2
Y = 4
MESH = pl.DeviceIdType.MESH


def kernel(
    n_wide, n_narrow,
    rows_ref, counts_ref, state_ref, down_ref, up_ref, bias_ref, grad_ref,
    crossed_ref, new_ref,
    raw, coded, ct, rows_all, pooled, passing, dense, down, up, bias, grad,
    rank_out, rank_in, ranks, cross_buf, grad_out, grad_pass, grad_in, row_out, row_in,
    load_sem, store_sem, send_sem, count_sem, row_sem, weight_sem, spread_sem, pass_sem,
    dense_sem, rank_sem, ranks_sem, back_sem, grad_sem, part_sem,
):
    f32, bf16 = jnp.float32, jnp.bfloat16
    Z, N = n_wide // Y, n_narrow
    half, pairs = Z // 2, N // 2
    block, cols = grad_ref.shape
    slots, rows_dev, emb = dense.shape[0], rows_ref.shape[1], rows_ref.shape[2]
    unit = Y * block
    w, n = lax.axis_index("wide"), lax.axis_index("narrow")
    z, y = w // Y, w % Y

    def shift(k, j):
        x, c = k // 2, k % 2
        if j == 0:
            near = jnp.where(x == 0, 0, half + x)
            return jnp.where(c == 0, half - x, near)
        return jnp.where(c == 0, 1 + x, Z - 1 - x)

    def unshift(d):
        j = jnp.where((d == 0) | ((d > pairs) & (d < Z - pairs)), 0, 1)
        c = jnp.where((d == 0) | (d > half), 1, 0)
        low = jnp.where(d > pairs, half - d, d - 1)
        high = jnp.where(d < Z - pairs, d - half, Z - 1 - d)
        x = jnp.where(d == 0, 0, jnp.where(d > half, high, low))
        return 2 * x + c, j

    pending = []

    def later(ref, i):
        pending.append(lambda: pltpu.make_async_copy(ref, ref, send_sem.at[i]).wait())

    def arrived(ref, sem):
        pltpu.make_async_copy(ref, ref, sem).wait()

    def remote(src, dst, i, sem, to):
        return pltpu.make_async_remote_copy(
            src_ref=src, dst_ref=dst, send_sem=send_sem.at[i], recv_sem=sem,
            device_id=to, device_id_type=MESH,
        )

    def finish():
        for wait in pending:
            wait()

    def load_unit(i, j):
        u = (z + shift((n + 1 + i) % N, j)) % Z
        pltpu.make_async_copy(
            counts_ref.at[0, :, pl.ds(pl.multiple_of(u * unit, unit), unit)], raw.at[u], load_sem.at[u]
        ).start()

    for j in range(2):
        pl.loop(0, N)(functools.partial(load_unit, j=j))
    first_col = pl.multiple_of(n * cols, cols)
    fixed = [
        pltpu.make_async_copy(bias_ref.at[:, pl.ds(first_col, cols)], bias, load_sem.at[Z]),
        pltpu.make_async_copy(grad_ref, grad, load_sem.at[Z + 1]),
        pltpu.make_async_copy(
            down_ref.at[pl.ds(pl.multiple_of(y * 16, 16), 16), pl.ds(first_col, cols)],
            down.at[y, n], load_sem.at[Z + 2]),
        pltpu.make_async_copy(
            up_ref.at[pl.ds(pl.multiple_of(z % Y * 16, 16), 16), pl.ds(first_col, cols)],
            up.at[z % Y, n], load_sem.at[Z + 3]),
    ]
    for copy in fixed:
        copy.start()

    barrier = pltpu.get_barrier_semaphore()

    @pl.loop(1, Y * N)
    def _(i):
        to = (y * N + n + i) % (Y * N)
        pl.semaphore_signal(barrier, inc=1, device_id=(z * Y + to // N, to % N), device_id_type=MESH)

    @pl.loop(1, Z)
    def _(i):
        pl.semaphore_signal(barrier, inc=1, device_id=((z + i) % Z * Y + y, n), device_id_type=MESH)

    def code_unit(i, j):
        u = (z + shift((n + 1 + i) % N, j)) % Z
        pltpu.make_async_copy(raw.at[u], raw.at[u], load_sem.at[u]).wait()
        coded[u] = raw[u].astype(f32).astype(bf16)

    pl.loop(0, N)(functools.partial(code_unit, j=0))
    rows_all[n] = rows_ref[0]
    pl.semaphore_wait(barrier, Y * N + Z - 2)

    @pl.loop(1, N)
    def _(i):
        k = (n + i) % N
        to_col = pl.multiple_of(k * cols, cols)
        remote(rows_ref.at[0], rows_all.at[n], 0, row_sem, (w, k)).start()
        remote(
            down_ref.at[pl.ds(pl.multiple_of(y * 16, 16), 16), pl.ds(to_col, cols)],
            down.at[y, n], 1, weight_sem.at[0], (w, k)).start()
        remote(
            up_ref.at[pl.ds(pl.multiple_of(z % Y * 16, 16), 16), pl.ds(to_col, cols)],
            up.at[z % Y, n], 2, weight_sem.at[1], (w, k)).start()

    def send_unit(i, j):
        k = (n + i) % N
        u = (z + shift(k, j)) % Z
        remote(coded.at[u], ct.at[j, n], 3 + j, count_sem.at[j], (w, k)).start()

    pl.loop(1, N)(functools.partial(send_unit, j=0))
    pl.loop(0, N)(functools.partial(code_unit, j=1))
    pl.loop(1, N)(functools.partial(send_unit, j=1))
    for j in range(2):
        ct[j, n] = coded[(z + shift(n, j)) % Z]
    later(rows_all.at[pl.ds(0, N - 1)], 0)
    later(down.at[0, pl.ds(0, N - 1)], 1)
    later(up.at[0, pl.ds(0, N - 1)], 2)
    for j in range(2):
        later(ct.at[j, pl.ds(0, N - 1)], 3 + j)

    for copy in fixed:
        copy.wait()
    arrived(down.at[y, pl.ds(0, N - 1)], weight_sem.at[0])
    for i in range(1, Y):
        remote(down.at[y], down.at[y], 5, spread_sem.at[0], (z * Y + (y + i) % Y, n)).start()
    later(down.at[pl.ds(0, Y - 1)], 5)
    arrived(up.at[z % Y, pl.ds(0, N - 1)], weight_sem.at[1])
    zq = z % Y
    for step in (1, Z - 1):
        remote(up.at[zq], up.at[zq], 6, spread_sem.at[1], ((z + step) % Z * Y + y, n)).start()
    for step, start in ((2, 0), (Z - 2, pairs)):
        part = up.at[zq, pl.ds(start, pairs)]
        remote(part, part, 6, spread_sem.at[1], ((z + step) % Z * Y + y, n)).start()
    later(up.at[pl.ds(0, Y - 1)], 6)

    arrived(rows_all.at[pl.ds(0, N - 1)], row_sem)
    table_rows = rows_all[...].reshape(N * rows_dev, emb)

    def along_z(src, dst, i, sem, far, to):
        @pl.when(far != 0)
        def _():
            remote(src, dst, i, sem, to).start()

        @pl.when(far == 0)
        def _():
            pltpu.make_async_copy(src, dst, sem).start()

        def wait():
            @pl.when(far != 0)
            def _():
                pltpu.make_async_copy(src, src, send_sem.at[i]).wait()

        pending.append(wait)

    def over_plane(src, dst, i, sem, to_w, to_n):
        is_me = (to_w == w) & (to_n == n)

        @pl.when(jnp.logical_not(is_me))
        def _():
            remote(src, dst, i, sem, (to_w, to_n)).start()

        @pl.when(is_me)
        def _():
            pltpu.make_async_copy(src, dst, sem).start()

        def wait():
            @pl.when(jnp.logical_not(is_me))
            def _():
                pltpu.make_async_copy(src, src, send_sem.at[i]).wait()

        pending.append(wait)

    for j in range(2):
        arrived(ct.at[j, pl.ds(0, N - 1)], count_sem.at[j])
        counts = ct[j].reshape(N * rows_dev, unit)
        pooled[j] = lax.dot_general(
            counts, table_rows, (((0,), (0,)), ((), ())), preferred_element_type=f32
        ).astype(bf16)
        far = shift(n, j)
        along_z(pooled.at[j], passing.at[j], 7 + j, pass_sem.at[j], far, ((z + far) % Z * Y + y, n))
    for j in range(2):
        arrived(passing.at[j], pass_sem.at[j])
        zt = (z + Z - shift(n, j)) % Z
        for i in range(Y):
            yd = (y + i) % Y
            over_plane(
                passing.at[j, pl.ds(pl.multiple_of(yd * block, 16), block)],
                dense.at[zt % 2 * Y + y], 9 + j * Y + i, dense_sem, z * Y + yd, zt // 2)

    arrived(down.at[pl.ds(0, Y - 1)], spread_sem.at[0])
    arrived(up.at[pl.ds(0, Y - 1)], spread_sem.at[1])
    arrived(dense, dense_sem)
    ranks_all = Y * N * 16
    dense_in = jnp.concatenate([dense[s] for s in range(slots)], axis=1)
    scaled = (grad[...].astype(f32) * dense_in.astype(f32)).astype(bf16)
    contract_cols = (((1,), (1,)), ((), ()))
    low = lax.dot_general(
        dense_in, down[...].reshape(ranks_all, cols), contract_cols, preferred_element_type=f32)
    rank_grad = lax.dot_general(
        scaled, up[...].reshape(ranks_all, cols), contract_cols, preferred_element_type=f32)
    for r in range(N // 2):
        rank_out[r] = low[:, r * emb:(r + 1) * emb].astype(bf16)
        rank_out[r + N // 2] = rank_grad[:, r * emb:(r + 1) * emb].astype(bf16)

    @pl.loop(1, N)
    def _(i):
        k = (n + i) % N
        remote(rank_out.at[k], rank_in.at[n], 17, rank_sem, (w, k)).start()

    later(rank_out.at[pl.ds(0, N - 1)], 17)
    rank_in[n] = rank_out[n]
    arrived(rank_in.at[pl.ds(0, N - 1)], rank_sem)
    ranks[n] = jnp.sum(rank_in[...].astype(f32), axis=0).astype(bf16)

    @pl.loop(1, N)
    def _(i):
        remote(ranks.at[n], ranks.at[n], 18, ranks_sem, (w, (n + i) % N)).start()

    later(ranks.at[pl.ds(0, N - 1)], 18)
    arrived(ranks.at[pl.ds(0, N - 1)], ranks_sem)
    low = jnp.concatenate([ranks[r] for r in range(N // 2)], axis=1)
    rank_grad = jnp.concatenate([ranks[r + N // 2] for r in range(N // 2)], axis=1)
    for s in range(slots):
        here = slice(s * emb, (s + 1) * emb)
        lifted = jnp.dot(
            low, down_cols(up, here, ranks_all), preferred_element_type=f32) + bias[:, here]
        back = jnp.dot(rank_grad, down_cols(down, here, ranks_all), preferred_element_type=f32)
        x = dense[s].astype(f32)
        grad_out[s] = (grad[:, here].astype(f32) * (lifted + 1.0) + back).astype(bf16)
        cross_buf[:, here] = (x * lifted + x).astype(bf16)
        zb, yt = s // Y, s % Y
        k, j = unshift((z + Z - (2 * n + zb)) % Z)
        over_plane(
            grad_out.at[s], grad_pass.at[j, pl.ds(pl.multiple_of(y * block, 16), block)],
            19 + s, back_sem.at[j], z * Y + yt, k)
    store = pltpu.make_async_copy(cross_buf, crossed_ref, store_sem)
    store.start()
    pending.append(store.wait)

    for j in range(2):
        arrived(grad_pass.at[j], back_sem.at[j])
        far = shift(n, j)
        along_z(
            grad_pass.at[j], grad_in.at[j], 27 + j, grad_sem.at[j], far,
            ((z + Z - far) % Z * Y + y, n))
    arrived(grad_in.at[0], grad_sem.at[0])
    part = jnp.dot(
        ct[0].reshape(N * rows_dev, unit), grad_in[0], preferred_element_type=f32)
    arrived(grad_in.at[1], grad_sem.at[1])
    part += jnp.dot(
        ct[1].reshape(N * rows_dev, unit), grad_in[1], preferred_element_type=f32)
    row_out[...] = part.reshape(N, rows_dev, emb)

    @pl.loop(1, N)
    def _(i):
        k = (n + i) % N
        remote(row_out.at[k], row_in.at[n], 29, part_sem, (w, k)).start()

    later(row_out.at[pl.ds(0, N - 1)], 29)
    row_in[n] = row_out[n]
    arrived(row_in.at[pl.ds(0, N - 1)], part_sem)
    row_grad = jnp.sum(row_in[...], axis=0)
    square = (rows_dev, rows_dev)
    diagonal = lax.broadcasted_iota(jnp.int32, square, 0) == lax.broadcasted_iota(jnp.int32, square, 1)
    state = jnp.sum(jnp.where(diagonal, state_ref[...], 0.0), axis=1, keepdims=True)
    state = state + jnp.mean(row_grad * row_grad, axis=1, keepdims=True)
    new_ref[0] = rows_ref[0].astype(f32) - learning_rate * row_grad / jnp.sqrt(state)
    finish()


def down_cols(ref, here, ranks_all):
    return ref[:, :, :, here].reshape(ranks_all, here.stop - here.start)


def on_device(gathered_rows, bag_counts, row_state, cross_down, cross_up, cross_bias, upstream):
    f32, bf16 = jnp.float32, jnp.bfloat16
    n_wide, n_narrow = lax.axis_size("wide"), lax.axis_size("narrow")
    Z, N = n_wide // Y, n_narrow
    rows_dev, emb = gathered_rows.shape[1:]
    block, cols = upstream.shape
    unit, slots = Y * block, cols // emb
    vmem = pl.BlockSpec(memory_space=pltpu.VMEM)
    hbm = pl.BlockSpec(memory_space=pl.ANY)
    dma = pltpu.SemaphoreType.DMA
    return pl.pallas_call(
        functools.partial(kernel, n_wide, n_narrow),
        out_shape=(
            jax.ShapeDtypeStruct((block, cols), bf16),
            jax.ShapeDtypeStruct((1, rows_dev, emb), f32),
        ),
        in_specs=[vmem, hbm, vmem, hbm, hbm, hbm, hbm],
        out_specs=(hbm, vmem),
        scratch_shapes=[
            pltpu.VMEM((Z, rows_dev, unit), jnp.int32),
            pltpu.VMEM((Z, rows_dev, unit), bf16),
            pltpu.VMEM((2, N, rows_dev, unit), bf16),
            pltpu.VMEM((N, rows_dev, emb), bf16),
            pltpu.VMEM((2, unit, emb), bf16),
            pltpu.VMEM((2, unit, emb), bf16),
            pltpu.VMEM((slots, block, emb), bf16),
            pltpu.VMEM((Y, N, 16, cols), bf16),
            pltpu.VMEM((Y, N, 16, cols), bf16),
            pltpu.VMEM((1, cols), f32),
            pltpu.VMEM((block, cols), bf16),
            pltpu.VMEM((N, block, emb), bf16),
            pltpu.VMEM((N, block, emb), bf16),
            pltpu.VMEM((N, block, emb), bf16),
            pltpu.VMEM((block, cols), bf16),
            pltpu.VMEM((slots, block, emb), bf16),
            pltpu.VMEM((2, unit, emb), bf16),
            pltpu.VMEM((2, unit, emb), bf16),
            pltpu.VMEM((N, rows_dev, emb), f32),
            pltpu.VMEM((N, rows_dev, emb), f32),
            dma((Z + 4,)), dma, dma((30,)), dma((2,)), dma, dma((2,)), dma((2,)), dma((2,)),
            dma, dma, dma, dma((2,)), dma((2,)), dma,
        ],
        compiler_params=pltpu.CompilerParams(
            collective_id=0, has_side_effects=True, vmem_limit_bytes=40 * 1024 * 1024
        ),
    )(
        gathered_rows, bag_counts, row_state, cross_down, cross_up,
        cross_bias.reshape(1, -1), upstream,
    )


def solution(mesh):
    placed = (
        P("wide", "narrow", None),
        P("wide", "narrow", None),
        P("wide", "narrow"),
        P("narrow", None),
        P("narrow", None),
        P(),
        P("wide", "narrow"),
    )
    return jax.shard_map(
        on_device,
        mesh=mesh,
        in_specs=placed,
        out_specs=(P("wide", "narrow"), P("wide", "narrow", None)),
        check_vma=False,
    )
```

```python
import functools
import types
import jax
import jax.numpy as jnp
from jax import lax
from jax.experimental import pallas as pl
from jax.experimental.pallas import tpu as pltpu
from jax.sharding import PartitionSpec as P

learning_rate = 0.2
Y = 4
RANK_ROWS = 16
MESH = pl.DeviceIdType.MESH


def split(block):
    first = -(-block // 64) * 32
    return first, block - first


def kernel(n_wide, n_narrow, names, *refs):
    m = types.SimpleNamespace(**dict(zip(names, refs, strict=True)))
    f32, bf16 = jnp.float32, jnp.bfloat16
    Z, N = n_wide // Y, n_narrow
    half, quarter = Z // 2, Z // 4
    block, cols = m.grad_ref.shape
    rows_dev, emb = m.rows_ref.shape[1:]
    slots = cols // emb
    unit, quad = Y * block, cols // Y
    per_quad = quad // emb
    ranks_all = Y * N * RANK_ROWS
    sizes = split(block)
    starts = (0, sizes[0])
    parts = range(2)
    w, n = lax.axis_index("wide"), lax.axis_index("narrow")
    z, y = w // Y, w % Y
    zq = z % Y

    def shift(k, j):
        x, c = k // 2, k % 2
        if j == 0:
            return jnp.where(c == 0, half - x, jnp.where(x == 0, Z - quarter, half + x))
        return jnp.where(
            c == 0, jnp.where(x == 0, quarter, x), jnp.where(x == 0, 0, Z - x))

    def unshift(d):
        e = jnp.where(d > half, Z - d, d)
        x = jnp.where(e == quarter, 0, jnp.where(e < quarter, e, half - e))
        c = jnp.where((d == 0) | (d > half), 1, 0)
        j = jnp.where((e > quarter) | (d == Z - quarter), 0, 1)
        return 2 * x + c, j

    pending = []
    used = [0]

    def new_send():
        used[0] += 1
        return m.send_sem.at[used[0] - 1]

    def wait_bytes(ref, sem):
        pltpu.make_async_copy(ref, ref, sem).wait()

    def later(ref, sem):
        pending.append(lambda: wait_bytes(ref, sem))

    def remote(src, dst, send, sem, to):
        return pltpu.make_async_remote_copy(
            src_ref=src, dst_ref=dst, send_sem=send, recv_sem=sem,
            device_id=to, device_id_type=MESH,
        )

    def move(src, dst, sem, here, to):
        send = new_send()

        @pl.when(jnp.logical_not(here))
        def _():
            remote(src, dst, send, sem, to).start()

        @pl.when(here)
        def _():
            pltpu.make_async_copy(src, dst, sem).start()

        def wait():
            @pl.when(jnp.logical_not(here))
            def _():
                wait_bytes(src, send)

        pending.append(wait)

    def finish():
        for wait in pending:
            wait()
        pending.clear()

    def load_unit(i, j):
        u = (z + shift((n + 1 + i) % N, j)) % Z
        pltpu.make_async_copy(
            m.counts_ref.at[0, :, pl.ds(pl.multiple_of(u * unit, unit), unit)],
            m.raw.at[u], m.load_sem.at[u],
        ).start()

    def chip_blocks(k):
        for which, ref in enumerate((m.down_ref, m.up_ref)):
            for q in range(Y):
                yield (
                    ref.at[:, :, pl.ds(pl.multiple_of(k * cols + q * quad, quad), quad)],
                    m.weights.at[which, q, :, n])

    pl.loop(0, N)(functools.partial(load_unit, j=0))
    fixed = [pltpu.make_async_copy(a, b, m.load_sem.at[Z + 2]) for a, b in chip_blocks(n)]
    own_blocks = m.weights.at[:, :, :, 0]

    def load_shares(k):
        for which, ref in enumerate((m.down_ref, m.up_ref)):
            pltpu.make_async_copy(
                ref.at[y, :, pl.ds(pl.multiple_of(k * cols + zq * quad, quad), quad)],
                m.shares.at[which, k], m.load_sem.at[Z + 3],
            ).start()

    small = [
        pltpu.make_async_copy(
            m.bias_ref.at[:, pl.ds(pl.multiple_of(n * cols, cols), cols)],
            m.bias, m.load_sem.at[Z]),
        pltpu.make_async_copy(m.grad_ref, m.grad, m.load_sem.at[Z + 1]),
    ]
    pl.loop(0, N)(load_shares)
    pl.loop(0, N)(functools.partial(load_unit, j=1))
    for copy in small + fixed:
        copy.start()

    barrier = pltpu.get_barrier_semaphore()

    @pl.loop(1, Y * N)
    def _(i):
        to = (y * N + n + i) % (Y * N)
        pl.semaphore_signal(barrier, inc=1, device_id=(z * Y + to // N, to % N), device_id_type=MESH)

    @pl.loop(1, Z)
    def _(i):
        pl.semaphore_signal(barrier, inc=1, device_id=((z + i) % Z * Y + y, n), device_id_type=MESH)

    @pl.loop(0, slots)
    def _(i):
        zt, yt = 2 * n + i // Y, i % Y
        k, _ = unshift((z + Z - zt) % Z)

        @pl.when(jnp.logical_not((zt == z) & (yt == y) & (k == n)))
        def _():
            pl.semaphore_signal(barrier, inc=1, device_id=(zt * Y + yt, k), device_id_type=MESH)

    pools_for_itself = jnp.where((shift(n, 1) == 0) & (z // 2 == n), 1, 0)

    def code_unit(i, j):
        u = (z + shift((n + 1 + i) % N, j)) % Z
        wait_bytes(m.raw.at[u], m.load_sem.at[u])
        values = m.raw[u].astype(f32)
        for h in parts:
            lanes = [
                values[:, a * block + starts[h]:a * block + starts[h] + sizes[h]] for a in range(Y)]
            m.coded[h][u] = jnp.concatenate(lanes, axis=1).astype(bf16)

    pl.loop(0, N)(functools.partial(code_unit, j=0))
    m.rows_all[n] = m.rows_ref[0]
    wait_bytes(m.shares, m.load_sem.at[Z + 3])
    pl.semaphore_wait(barrier, Y * N + Z - 2 + slots - pools_for_itself)

    sends = [new_send() for _ in range(3)]

    @pl.loop(2, N)
    def _(i):
        k = (n // 2 * 2 + i) % N
        remote(m.shares.at[:, k], m.weights.at[:, zq, y, n], sends[1], m.column_sem.at[0], (w, k)).start()

    @pl.loop(1, N)
    def _(i):
        remote(m.rows_ref.at[0], m.rows_all.at[n], sends[0], m.row_sem, (w, (n + i) % N)).start()

    later(m.rows_all.at[pl.ds(0, N - 1)], sends[0])
    later(m.weights.at[:, 0, 0, pl.ds(0, N - 2)], sends[1])

    def to_sibling():
        sibling = (w, n + 1 - 2 * (n % 2))
        for a, b in chip_blocks(sibling[1]):
            remote(a, b, sends[2], m.sibling_sem, sibling).start()
        later(own_blocks, sends[2])

    others = [pl.ds((n // 2 + i) % (N // 2) * 2, 2) for i in range(1, N // 2)]

    def spread_columns():
        wait_bytes(m.weights.at[:, 0, 0, pl.ds(0, N - 2)], m.column_sem.at[0])
        send = new_send()
        for step in (1, Z - 1, 2, Z - 2):
            for ds in others:
                part = m.weights.at[:, zq, y, ds]
                if step in (2, Z - 2):
                    part = m.weights.at[0 if step == 2 else 1, zq, y, ds]
                remote(part, part, send, m.column_sem.at[1], ((z + step) % Z * Y + y, n)).start()
        later(m.weights.at[:, pl.ds(0, Y - 1), 0, pl.ds(0, N - 2)], send)

    def spread_ranks():
        wait_bytes(m.weights.at[:, pl.ds(0, Y - 1), 0, pl.ds(0, N - 2)], m.column_sem.at[1])
        for which in range(2):
            send = new_send()
            for step in (1, Y - 1):
                for ds in others:
                    part = m.weights.at[which, :, y, ds]
                    remote(
                        part, part, send, m.rank_block_sem.at[which, 0], (z * Y + (y + step) % Y, n)
                    ).start()
            later(m.weights.at[which, :, pl.ds(0, 2), pl.ds(0, N - 2)], send)

    def forward_ranks(which):
        wait_bytes(m.weights.at[which, :, pl.ds(0, 2), pl.ds(0, N - 2)], m.rank_block_sem.at[which, 0])
        send = new_send()
        for step, start in ((1, 0), (Y - 1, Y // 2)):
            for ds in others:
                part = m.weights.at[which, pl.ds(start, Y // 2), (y + Y - step) % Y, ds]
                remote(
                    part, part, send, m.rank_block_sem.at[which, 1], (z * Y + (y + step) % Y, n)
                ).start()
        later(m.weights.at[which, :, 0, pl.ds(0, N - 2)], send)

    def weights_here(which):
        wait_bytes(m.weights.at[which, :, 0, pl.ds(0, N - 2)], m.rank_block_sem.at[which, 1])

    def small_here():
        wait_bytes(own_blocks, m.sibling_sem)
        for copy in small + fixed:
            copy.wait()

    def send_units(h, j):
        send = new_send()

        @pl.loop(1, N)
        def _(i):
            k = (n + i) % N
            u = (z + shift(k, j)) % Z
            remote(m.coded[h].at[u], m.ct[h].at[j, n], send, m.count_sem.at[h, j], (w, k)).start()

        later(m.ct[h].at[j, pl.ds(0, N - 1)], send)

    spread_columns()
    send_units(0, 0)
    pl.loop(0, N)(functools.partial(code_unit, j=1))
    send_units(0, 1)
    to_sibling()
    spread_ranks()
    send_units(1, 0)
    send_units(1, 1)
    for h in parts:
        for j in range(2):
            m.ct[h][j, n] = m.coded[h][(z + shift(n, j)) % Z]

    def pool(h, j):
        wait_bytes(m.ct[h].at[j, pl.ds(0, N - 1)], m.count_sem.at[h, j])
        counts = m.ct[h][j].reshape(N * rows_dev, Y * sizes[h])
        table_rows = m.rows_all[...].reshape(N * rows_dev, emb)
        m.pooled[h][j] = lax.dot_general(
            counts, table_rows, (((0,), (0,)), ((), ())), preferred_element_type=f32
        ).astype(bf16)
        far = shift(n, j)
        zw = (z + far) % Z
        size = sizes[h]
        for i in range(Y):
            yd = (y + i) % Y
            move(
                m.pooled[h].at[j, pl.ds(pl.multiple_of(yd * size, 16), size)],
                m.dense[h].at[z % 2 * Y + y], m.dense_sem.at[h],
                (yd == y) & (z // 2 == n) & (zw == z), (zw * Y + yd, z // 2))

    def to_ranks(h):
        wait_bytes(m.dense[h], m.dense_sem.at[h])
        rows = pl.ds(starts[h], sizes[h])
        width = ranks_all * 2 // N
        send = new_send()
        for which in range(2):
            if h == 0:
                weights_here(which)
            total = 0.0
            for q in range(Y):
                x = jnp.concatenate(
                    [m.dense[h][q * per_quad + s] for s in range(per_quad)], axis=1)
                if which == 1:
                    slope = m.grad[rows, q * quad:(q + 1) * quad].astype(f32)
                    x = (slope * x.astype(f32)).astype(bf16)
                total += lax.dot_general(
                    x, m.weights[which, q].reshape(ranks_all, quad), (((1,), (1,)), ((), ())),
                    preferred_element_type=f32)
            first = which * (N // 2)
            for r in range(N // 2):
                m.rank_out[h][first + r] = total[:, r * width:(r + 1) * width].astype(bf16)

            @pl.loop(0, N // 2)
            def _(i):
                k = first + (n + i) % (N // 2)

                @pl.when(k != n)
                def _():
                    remote(
                        m.rank_out[h].at[k], m.rank_in[h].at[n], send, m.rank_sem.at[h], (w, k)
                    ).start()

        later(m.rank_out[h].at[pl.ds(0, N - 1)], send)
        m.rank_in[h][n] = m.rank_out[h][n]

    def sum_ranks(h):
        wait_bytes(m.rank_in[h].at[pl.ds(0, N - 1)], m.rank_sem.at[h])
        m.ranks[h][n] = jnp.sum(m.rank_in[h][...].astype(f32), axis=0).astype(bf16)
        send = new_send()

        @pl.loop(1, N)
        def _(i):
            remote(
                m.ranks[h].at[n], m.ranks[h].at[n], send, m.ranks_sem.at[h], (w, (n + i) % N)
            ).start()

        later(m.ranks[h].at[pl.ds(0, N - 1)], send)

    def from_ranks(h):
        wait_bytes(m.ranks[h].at[pl.ds(0, N - 1)], m.ranks_sem.at[h])
        size = sizes[h]
        rows = pl.ds(starts[h], size)
        low = jnp.concatenate([m.ranks[h][r] for r in range(N // 2)], axis=1)
        rank_grad = jnp.concatenate([m.ranks[h][r] for r in range(N // 2, N)], axis=1)
        for q in range(Y):
            here = slice(q * quad, (q + 1) * quad)
            lifted = jnp.dot(
                low, m.weights[1, q].reshape(ranks_all, quad), preferred_element_type=f32) + m.bias[:, here]
            back = jnp.dot(
                rank_grad, m.weights[0, q].reshape(ranks_all, quad), preferred_element_type=f32)
            x = jnp.concatenate(
                [m.dense[h][q * per_quad + s] for s in range(per_quad)], axis=1).astype(f32)
            slope = (m.grad[rows, here].astype(f32) * (lifted + 1.0) + back).astype(bf16)
            m.cross_buf[rows, here] = (x * lifted + x).astype(bf16)
            for s in range(per_quad):
                slot = q * per_quad + s
                m.grad_out[h][slot] = slope[:, s * emb:(s + 1) * emb]
                k, j = unshift((z + Z - (2 * n + slot // Y)) % Z)
                yt = slot % Y
                move(
                    m.grad_out[h].at[slot],
                    m.grad_pass[h].at[j, pl.ds(pl.multiple_of(y * size, 16), size)],
                    m.back_sem.at[h, j], (yt == y) & (k == n), (z * Y + yt, k))
        store = pltpu.make_async_copy(m.cross_buf.at[rows], m.crossed_ref.at[rows], m.store_sem.at[h])
        store.start()
        pending.append(store.wait)

    def pass_back(h, j):
        wait_bytes(m.grad_pass[h].at[j], m.back_sem.at[h, j])
        far = shift(n, j)
        move(
            m.grad_pass[h].at[j], m.grad_in[h].at[j], m.grad_sem.at[h, j],
            far == 0, ((z + Z - far) % Z * Y + y, n))

    def row_part(h, j):
        wait_bytes(m.grad_in[h].at[j], m.grad_sem.at[h, j])
        return jnp.dot(
            m.ct[h][j].reshape(N * rows_dev, Y * sizes[h]), m.grad_in[h][j],
            preferred_element_type=f32)

    wait_bytes(m.rows_all.at[pl.ds(0, N - 1)], m.row_sem)
    pool(0, 0)
    pool(0, 1)
    forward_ranks(0)
    pool(1, 0)
    forward_ranks(1)
    pool(1, 1)
    small_here()
    to_ranks(0)
    sum_ranks(0)
    to_ranks(1)
    from_ranks(0)
    sum_ranks(1)
    pass_back(0, 0)
    pass_back(0, 1)
    from_ranks(1)
    pass_back(1, 0)
    pass_back(1, 1)
    part = row_part(0, 0) + row_part(0, 1)
    part += row_part(1, 0)
    part += row_part(1, 1)
    m.row_out[...] = part.astype(bf16).reshape(N, rows_dev, emb)
    last = new_send()

    @pl.loop(1, N)
    def _(i):
        k = (n + i) % N
        remote(m.row_out.at[k], m.row_in.at[n], last, m.part_sem, (w, k)).start()

    m.row_in[n] = m.row_out[n]
    square = (rows_dev, rows_dev)
    diagonal = lax.broadcasted_iota(jnp.int32, square, 0) == lax.broadcasted_iota(jnp.int32, square, 1)
    state = jnp.sum(jnp.where(diagonal, m.state_ref[...], 0.0), axis=1, keepdims=True)
    finish()
    wait_bytes(m.row_in.at[pl.ds(0, N - 1)], m.part_sem)
    row_grad = jnp.sum(m.row_in[...].astype(f32), axis=0)
    state = state + jnp.mean(row_grad * row_grad, axis=1, keepdims=True)
    m.new_ref[0] = m.rows_ref[0].astype(f32) - learning_rate * row_grad / jnp.sqrt(state)
    wait_bytes(m.row_out.at[pl.ds(0, N - 1)], last)


def on_device(gathered_rows, bag_counts, row_state, cross_down, cross_up, cross_bias, upstream):
    f32, bf16 = jnp.float32, jnp.bfloat16
    n_wide, N = lax.axis_size("wide"), lax.axis_size("narrow")
    Z = n_wide // Y
    rows_dev, emb = gathered_rows.shape[1:]
    block, cols = upstream.shape
    unit, slots = Y * block, cols // emb
    width = 2 * cross_down.shape[0]
    sizes = split(block)
    vmem = pl.BlockSpec(memory_space=pltpu.VMEM)
    hbm = pl.BlockSpec(memory_space=pl.ANY)
    dma = pltpu.SemaphoreType.DMA

    def both(shape_of, dtype=bf16):
        return tuple(pltpu.VMEM(shape_of(size), dtype) for size in sizes)

    scratch = dict(
        raw=pltpu.VMEM((Z, rows_dev, unit), jnp.int32),
        coded=both(lambda size: (Z, rows_dev, Y * size)),
        ct=both(lambda size: (2, N, rows_dev, Y * size)),
        rows_all=pltpu.VMEM((N, rows_dev, emb), bf16),
        pooled=both(lambda size: (2, Y * size, emb)),
        dense=both(lambda size: (slots, size, emb)),
        weights=pltpu.VMEM((2, Y, Y, N, RANK_ROWS, cols // Y), bf16),
        shares=pltpu.VMEM((2, N, RANK_ROWS, cols // Y), bf16),
        bias=pltpu.VMEM((1, cols), f32),
        grad=pltpu.VMEM((block, cols), bf16),
        rank_out=both(lambda size: (N, size, width)),
        rank_in=both(lambda size: (N, size, width)),
        ranks=both(lambda size: (N, size, width)),
        cross_buf=pltpu.VMEM((block, cols), bf16),
        grad_out=both(lambda size: (slots, size, emb)),
        grad_pass=both(lambda size: (2, Y * size, emb)),
        grad_in=both(lambda size: (2, Y * size, emb)),
        row_out=pltpu.VMEM((N, rows_dev, emb), bf16),
        row_in=pltpu.VMEM((N, rows_dev, emb), bf16),
        load_sem=dma((Z + 4,)), store_sem=dma((2,)), send_sem=dma((64,)),
        count_sem=dma((2, 2)), row_sem=dma, column_sem=dma((2,)), rank_block_sem=dma((2, 2)),
        dense_sem=dma((2,)), rank_sem=dma((2,)), ranks_sem=dma((2,)),
        back_sem=dma((2, 2)), grad_sem=dma((2, 2)), part_sem=dma, sibling_sem=dma,
    )
    names = (
        "rows_ref", "counts_ref", "state_ref", "down_ref", "up_ref", "bias_ref", "grad_ref",
        "crossed_ref", "new_ref", *scratch)
    return pl.pallas_call(
        functools.partial(kernel, n_wide, N, names),
        out_shape=(
            jax.ShapeDtypeStruct((block, cols), bf16),
            jax.ShapeDtypeStruct((1, rows_dev, emb), f32),
        ),
        in_specs=[vmem, hbm, vmem, hbm, hbm, hbm, hbm],
        out_specs=(hbm, vmem),
        scratch_shapes=tuple(scratch.values()),
        compiler_params=pltpu.CompilerParams(
            collective_id=0, has_side_effects=True, vmem_limit_bytes=60 * 1024 * 1024
        ),
    )(
        gathered_rows, bag_counts, row_state, cross_down.reshape(Y, RANK_ROWS, -1),
        cross_up.reshape(Y, RANK_ROWS, -1), cross_bias.reshape(1, -1), upstream,
    )


def solution(mesh):
    placed = (
        P("wide", "narrow", None),
        P("wide", "narrow", None),
        P("wide", "narrow"),
        P("narrow", None),
        P("narrow", None),
        P(),
        P("wide", "narrow"),
    )
    return jax.shard_map(
        on_device,
        mesh=mesh,
        in_specs=placed,
        out_specs=(P("wide", "narrow"), P("wide", "narrow", None)),
        check_vma=False,
    )
```

```python
import functools
import types
import jax
import jax.numpy as jnp
from jax import lax
from jax.experimental import pallas as pl
from jax.experimental.pallas import tpu as pltpu
from jax.sharding import PartitionSpec as P

learning_rate = 0.2
Y = 4
RANK_ROWS = 16
MESH = pl.DeviceIdType.MESH


def split(block):
    most = -(-block // 96) * 32
    return tuple(min(most, block - first) for first in range(0, block, most))


def kernel(n_wide, n_narrow, names, *refs):
    m = types.SimpleNamespace(**dict(zip(names, refs, strict=True)))
    f32, bf16 = jnp.float32, jnp.bfloat16
    Z, N = n_wide // Y, n_narrow
    half, quarter = Z // 2, Z // 4
    block, cols = m.grad_ref.shape
    rows_dev, emb = m.rows_ref.shape[1:]
    slots = cols // emb
    unit, quad = Y * block, cols // Y
    per_quad = quad // emb
    ranks_all = Y * N * RANK_ROWS
    sizes = split(block)
    starts = [sum(sizes[:h]) for h in range(len(sizes))]
    parts = range(len(sizes))
    w, n = lax.axis_index("wide"), lax.axis_index("narrow")
    z, y = w // Y, w % Y
    zq = z % Y

    def shift(k, j):
        x, c = k // 2, k % 2
        if j == 0:
            return jnp.where(c == 0, half - x, jnp.where(x == 0, Z - quarter, half + x))
        return jnp.where(
            c == 0, jnp.where(x == 0, quarter, x), jnp.where(x == 0, 0, Z - x))

    def unshift(d):
        e = jnp.where(d > half, Z - d, d)
        x = jnp.where(e == quarter, 0, jnp.where(e < quarter, e, half - e))
        c = jnp.where((d == 0) | (d > half), 1, 0)
        j = jnp.where((e > quarter) | (d == Z - quarter), 0, 1)
        return 2 * x + c, j

    pending = []
    used = [0]

    def new_send():
        used[0] += 1
        return m.send_sem.at[used[0] - 1]

    def wait_bytes(ref, sem):
        pltpu.make_async_copy(ref, ref, sem).wait()

    def later(ref, sem):
        pending.append(lambda: wait_bytes(ref, sem))

    def remote(src, dst, send, sem, to):
        return pltpu.make_async_remote_copy(
            src_ref=src, dst_ref=dst, send_sem=send, recv_sem=sem,
            device_id=to, device_id_type=MESH,
        )

    def move(src, dst, sem, here, to):
        send = new_send()

        @pl.when(jnp.logical_not(here))
        def _():
            remote(src, dst, send, sem, to).start()

        @pl.when(here)
        def _():
            pltpu.make_async_copy(src, dst, sem).start()

        def wait():
            @pl.when(jnp.logical_not(here))
            def _():
                wait_bytes(src, send)

        pending.append(wait)

    def finish():
        for wait in pending:
            wait()
        pending.clear()

    def load_unit(i, j):
        u = (z + shift((n + 1 + i) % N, j)) % Z
        pltpu.make_async_copy(
            m.counts_ref.at[0, :, pl.ds(pl.multiple_of(u * unit, unit), unit)],
            m.raw.at[u], m.load_sem.at[u],
        ).start()

    def chip_blocks(k):
        for which, ref in enumerate((m.down_ref, m.up_ref)):
            for q in range(Y):
                yield (
                    ref.at[:, :, pl.ds(pl.multiple_of(k * cols + q * quad, quad), quad)],
                    m.weights.at[which, q, :, n])

    pl.loop(0, N)(functools.partial(load_unit, j=0))
    fixed = [pltpu.make_async_copy(a, b, m.load_sem.at[Z + 2]) for a, b in chip_blocks(n)]
    own_blocks = m.weights.at[:, :, :, 0]

    def load_shares(k):
        def load(ref, q, into):
            first = pl.multiple_of(k * cols + q * quad, quad)
            pltpu.make_async_copy(
                ref.at[y, :, pl.ds(first, quad)], into, m.load_sem.at[Z + 3]).start()

        for q in range(Y):
            load(m.down_ref, q, m.down_share.at[k, q])
        load(m.up_ref, zq, m.up_share.at[k])

    small = [
        pltpu.make_async_copy(
            m.bias_ref.at[:, pl.ds(pl.multiple_of(n * cols, cols), cols)],
            m.bias, m.load_sem.at[Z]),
        pltpu.make_async_copy(m.grad_ref, m.grad, m.load_sem.at[Z + 1]),
    ]
    pl.loop(0, N)(load_shares)
    pl.loop(0, N)(functools.partial(load_unit, j=1))
    for copy in small + fixed:
        copy.start()

    barrier = pltpu.get_barrier_semaphore()

    @pl.loop(1, Y * N)
    def _(i):
        to = (y * N + n + i) % (Y * N)
        pl.semaphore_signal(barrier, inc=1, device_id=(z * Y + to // N, to % N), device_id_type=MESH)

    for step in (1, 2, Z - 2, Z - 1):
        pl.semaphore_signal(barrier, inc=1, device_id=((z + step) % Z * Y + y, n), device_id_type=MESH)

    for j in range(2):
        @pl.when(shift(n, j) != 0)
        def _():
            to = (z + shift(n, j)) % Z * Y + y
            pl.semaphore_signal(barrier, inc=1, device_id=(to, n), device_id_type=MESH)

    @pl.loop(0, slots)
    def _(i):
        zt, yt = 2 * n + i // Y, i % Y
        k, _ = unshift((z + Z - zt) % Z)

        @pl.when(jnp.logical_not((zt == z) & (yt == y) & (k == n)))
        def _():
            pl.semaphore_signal(barrier, inc=1, device_id=(zt * Y + yt, k), device_id_type=MESH)

    pools_for_itself = jnp.where((shift(n, 1) == 0) & (z // 2 == n), 1, 0)

    def code_unit(i, j):
        u = (z + shift((n + 1 + i) % N, j)) % Z
        wait_bytes(m.raw.at[u], m.load_sem.at[u])
        values = m.raw[u].astype(f32)
        for h in parts:
            lanes = [
                values[:, a * block + starts[h]:a * block + starts[h] + sizes[h]] for a in range(Y)]
            m.coded[h][u] = jnp.concatenate(lanes, axis=1).astype(bf16)

    pl.loop(0, N)(functools.partial(code_unit, j=0))
    m.rows_all[n] = m.rows_ref[0]
    wait_bytes(m.down_share, m.load_sem.at[Z + 3])
    wait_bytes(m.up_share, m.load_sem.at[Z + 3])
    pl.semaphore_wait(
        barrier, Y * N + 5 + slots - pools_for_itself - jnp.where(shift(n, 1) == 0, 1, 0))

    sends = [new_send() for _ in range(4)]

    @pl.loop(2, N)
    def _(i):
        k = (n // 2 * 2 + i) % N
        remote(
            m.down_share.at[k], m.weights.at[0, :, y, n], sends[1], m.column_sem.at[0], (w, k)
        ).start()

    @pl.loop(2, N)
    def _(i):
        k = (n // 2 * 2 + i) % N
        remote(
            m.up_share.at[k], m.weights.at[1, zq, y, n], sends[3], m.column_sem.at[2], (w, k)
        ).start()

    @pl.loop(1, N)
    def _(i):
        remote(m.rows_ref.at[0], m.rows_all.at[n], sends[0], m.row_sem, (w, (n + i) % N)).start()

    later(m.rows_all.at[pl.ds(0, N - 1)], sends[0])
    later(m.weights.at[0, :, 0, pl.ds(0, N - 2)], sends[1])
    later(m.weights.at[1, 0, 0, pl.ds(0, N - 2)], sends[3])

    def to_sibling():
        sibling = (w, n + 1 - 2 * (n % 2))
        for a, b in chip_blocks(sibling[1]):
            remote(a, b, sends[2], m.sibling_sem, sibling).start()
        later(own_blocks, sends[2])

    others = [(n // 2 + i) % (N // 2) * 2 for i in range(1, N // 2)]

    def spread_columns():
        wait_bytes(m.weights.at[1, 0, 0, pl.ds(0, N - 2)], m.column_sem.at[2])
        send = new_send()
        for step in (1, Z - 1, 2, Z - 2):
            for k in others:
                part = m.weights.at[1, zq, y, pl.ds(k, 2)]
                if step in (2, Z - 2):
                    part = m.weights.at[1, zq, y, k + (0 if step == 2 else 1)]
                remote(part, part, send, m.column_sem.at[1], ((z + step) % Z * Y + y, n)).start()
        later(m.weights.at[1, pl.ds(0, Y - 1), 0, pl.ds(0, N - 2)], send)

    def spread_ranks(which):
        if which == 0:
            wait_bytes(m.weights.at[0, :, 0, pl.ds(0, N - 2)], m.column_sem.at[0])
        else:
            wait_bytes(m.weights.at[1, pl.ds(0, Y - 1), 0, pl.ds(0, N - 2)], m.column_sem.at[1])
        send = new_send()
        for step in (1, Y - 1):
            for k in others:
                part = m.weights.at[which, :, y, pl.ds(k, 2)]
                remote(
                    part, part, send, m.rank_block_sem.at[which, 0], (z * Y + (y + step) % Y, n)
                ).start()
        later(m.weights.at[which, :, pl.ds(0, 2), pl.ds(0, N - 2)], send)

    def forward_ranks(which):
        wait_bytes(m.weights.at[which, :, pl.ds(0, 2), pl.ds(0, N - 2)], m.rank_block_sem.at[which, 0])
        send = new_send()
        for step, start in ((1, 0), (Y - 1, Y // 2)):
            for k in others:
                part = m.weights.at[which, pl.ds(start, Y // 2), (y + Y - step) % Y, pl.ds(k, 2)]
                remote(
                    part, part, send, m.rank_block_sem.at[which, 1], (z * Y + (y + step) % Y, n)
                ).start()
        later(m.weights.at[which, :, 0, pl.ds(0, N - 2)], send)

    def weights_here(which):
        wait_bytes(m.weights.at[which, :, 0, pl.ds(0, N - 2)], m.rank_block_sem.at[which, 1])

    def small_here():
        wait_bytes(own_blocks, m.sibling_sem)
        for copy in small + fixed:
            copy.wait()

    def send_units(h, j):
        send = new_send()

        @pl.loop(1, N)
        def _(i):
            k = (n + i) % N
            u = (z + shift(k, j)) % Z
            remote(m.coded[h].at[u], m.ct[h].at[j, n], send, m.count_sem.at[h, j], (w, k)).start()

        later(m.ct[h].at[j, pl.ds(0, N - 1)], send)

    send_units(0, 0)
    pl.loop(0, N)(functools.partial(code_unit, j=1))
    send_units(0, 1)
    spread_ranks(0)
    spread_columns()
    for h in parts[1:]:
        send_units(h, 0)
        send_units(h, 1)
    to_sibling()
    for h in parts:
        for j in range(2):
            m.ct[h][j, n] = m.coded[h][(z + shift(n, j)) % Z]

    def pool(h, j):
        wait_bytes(m.ct[h].at[j, pl.ds(0, N - 1)], m.count_sem.at[h, j])
        counts = m.ct[h][j].reshape(N * rows_dev, Y * sizes[h])
        table_rows = m.rows_all[...].reshape(N * rows_dev, emb)
        m.pooled[h][j] = lax.dot_general(
            counts, table_rows, (((0,), (0,)), ((), ())), preferred_element_type=f32
        ).astype(bf16)
        far = shift(n, j)
        zw = (z + far) % Z
        size = sizes[h]
        for i in range(Y):
            yd = (y + i) % Y
            move(
                m.pooled[h].at[j, pl.ds(pl.multiple_of(yd * size, 16), size)],
                m.dense[h].at[z % 2 * Y + y], m.dense_sem.at[h],
                (yd == y) & (z // 2 == n) & (zw == z), (zw * Y + yd, z // 2))

    def to_ranks(h):
        wait_bytes(m.dense[h], m.dense_sem.at[h])
        rows = pl.ds(starts[h], sizes[h])
        width = ranks_all * 2 // N
        send = new_send()
        for which in range(2):
            if h == 0:
                weights_here(which)
            total = 0.0
            for q in range(Y):
                x = jnp.concatenate(
                    [m.dense[h][q * per_quad + s] for s in range(per_quad)], axis=1)
                if which == 1:
                    slope = m.grad[rows, q * quad:(q + 1) * quad].astype(f32)
                    x = (slope * x.astype(f32)).astype(bf16)
                total += lax.dot_general(
                    x, m.weights[which, q].reshape(ranks_all, quad), (((1,), (1,)), ((), ())),
                    preferred_element_type=f32)
            first = which * (N // 2)
            for r in range(N // 2):
                m.rank_out[h][first + r] = total[:, r * width:(r + 1) * width].astype(bf16)

            @pl.loop(0, N // 2)
            def _(i):
                k = first + (n + i) % (N // 2)

                @pl.when(k != n)
                def _():
                    remote(
                        m.rank_out[h].at[k], m.rank_in[h].at[n], send, m.rank_sem.at[h], (w, k)
                    ).start()

        later(m.rank_out[h].at[pl.ds(0, N - 1)], send)
        m.rank_in[h][n] = m.rank_out[h][n]

    def sum_ranks(h):
        wait_bytes(m.rank_in[h].at[pl.ds(0, N - 1)], m.rank_sem.at[h])
        m.ranks[h][n] = jnp.sum(m.rank_in[h][...].astype(f32), axis=0).astype(bf16)
        send = new_send()

        @pl.loop(1, N)
        def _(i):
            remote(
                m.ranks[h].at[n], m.ranks[h].at[n], send, m.ranks_sem.at[h], (w, (n + i) % N)
            ).start()

        later(m.ranks[h].at[pl.ds(0, N - 1)], send)

    def from_ranks(h):
        wait_bytes(m.ranks[h].at[pl.ds(0, N - 1)], m.ranks_sem.at[h])
        size = sizes[h]
        rows = pl.ds(starts[h], size)
        low = jnp.concatenate([m.ranks[h][r] for r in range(N // 2)], axis=1)
        rank_grad = jnp.concatenate([m.ranks[h][r] for r in range(N // 2, N)], axis=1)
        for q in range(Y):
            here = slice(q * quad, (q + 1) * quad)
            lifted = jnp.dot(
                low, m.weights[1, q].reshape(ranks_all, quad), preferred_element_type=f32) + m.bias[:, here]
            back = jnp.dot(
                rank_grad, m.weights[0, q].reshape(ranks_all, quad), preferred_element_type=f32)
            x = jnp.concatenate(
                [m.dense[h][q * per_quad + s] for s in range(per_quad)], axis=1).astype(f32)
            slope = (m.grad[rows, here].astype(f32) * (lifted + 1.0) + back).astype(bf16)
            m.cross_buf[rows, here] = (x * lifted + x).astype(bf16)
            for s in range(per_quad):
                slot = q * per_quad + s
                m.grad_out[h][slot] = slope[:, s * emb:(s + 1) * emb]
                k, j = unshift((z + Z - (2 * n + slot // Y)) % Z)
                yt = slot % Y
                move(
                    m.grad_out[h].at[slot],
                    m.grad_pass[h].at[j, pl.ds(pl.multiple_of(y * size, 16), size)],
                    m.back_sem.at[h, j], (yt == y) & (k == n), (z * Y + yt, k))
        store = pltpu.make_async_copy(m.cross_buf.at[rows], m.crossed_ref.at[rows], m.store_sem.at[h])
        store.start()
        pending.append(store.wait)

    def pass_back(h, j):
        wait_bytes(m.grad_pass[h].at[j], m.back_sem.at[h, j])
        far = shift(n, j)
        move(
            m.grad_pass[h].at[j], m.grad_in[h].at[j], m.grad_sem.at[h, j],
            far == 0, ((z + Z - far) % Z * Y + y, n))

    def row_part(h, j):
        wait_bytes(m.grad_in[h].at[j], m.grad_sem.at[h, j])
        return jnp.dot(
            m.ct[h][j].reshape(N * rows_dev, Y * sizes[h]), m.grad_in[h][j],
            preferred_element_type=f32)

    wait_bytes(m.rows_all.at[pl.ds(0, N - 1)], m.row_sem)
    spread_ranks(1)
    pool(0, 0)
    pool(0, 1)
    forward_ranks(0)
    pool(1, 0)
    forward_ranks(1)
    pool(1, 1)
    for h in parts[2:]:
        pool(h, 0)
        pool(h, 1)
    small_here()

    def step_back(h):
        pass_back(h, 0)
        pass_back(h, 1)

    to_ranks(0)
    for h in parts:
        sum_ranks(h)
        if h + 1 < len(sizes):
            to_ranks(h + 1)
        if h > 0:
            step_back(h - 1)
        from_ranks(h)
    step_back(parts[-1])
    part = 0.0
    for h in parts:
        part += row_part(h, 0) + row_part(h, 1)
    m.row_out[...] = part.astype(bf16).reshape(N, rows_dev, emb)
    last = new_send()

    @pl.loop(1, N)
    def _(i):
        k = (n + i) % N
        remote(m.row_out.at[k], m.row_in.at[n], last, m.part_sem, (w, k)).start()

    m.row_in[n] = m.row_out[n]
    square = (rows_dev, rows_dev)
    diagonal = lax.broadcasted_iota(jnp.int32, square, 0) == lax.broadcasted_iota(jnp.int32, square, 1)
    state = jnp.sum(jnp.where(diagonal, m.state_ref[...], 0.0), axis=1, keepdims=True)
    finish()
    wait_bytes(m.row_in.at[pl.ds(0, N - 1)], m.part_sem)
    row_grad = jnp.sum(m.row_in[...].astype(f32), axis=0)
    state = state + jnp.mean(row_grad * row_grad, axis=1, keepdims=True)
    m.new_ref[0] = m.rows_ref[0].astype(f32) - learning_rate * row_grad / jnp.sqrt(state)
    wait_bytes(m.row_out.at[pl.ds(0, N - 1)], last)


def on_device(gathered_rows, bag_counts, row_state, cross_down, cross_up, cross_bias, upstream):
    f32, bf16 = jnp.float32, jnp.bfloat16
    n_wide, N = lax.axis_size("wide"), lax.axis_size("narrow")
    Z = n_wide // Y
    rows_dev, emb = gathered_rows.shape[1:]
    block, cols = upstream.shape
    unit, slots = Y * block, cols // emb
    width = 2 * cross_down.shape[0]
    sizes = split(block)
    n_parts = len(sizes)
    vmem = pl.BlockSpec(memory_space=pltpu.VMEM)
    hbm = pl.BlockSpec(memory_space=pl.ANY)
    dma = pltpu.SemaphoreType.DMA

    def each(shape_of, dtype=bf16):
        return tuple(pltpu.VMEM(shape_of(size), dtype) for size in sizes)

    scratch = dict(
        raw=pltpu.VMEM((Z, rows_dev, unit), jnp.int32),
        coded=each(lambda size: (Z, rows_dev, Y * size)),
        ct=each(lambda size: (2, N, rows_dev, Y * size)),
        rows_all=pltpu.VMEM((N, rows_dev, emb), bf16),
        pooled=each(lambda size: (2, Y * size, emb)),
        dense=each(lambda size: (slots, size, emb)),
        weights=pltpu.VMEM((2, Y, Y, N, RANK_ROWS, cols // Y), bf16),
        down_share=pltpu.VMEM((N, Y, RANK_ROWS, cols // Y), bf16),
        up_share=pltpu.VMEM((N, RANK_ROWS, cols // Y), bf16),
        bias=pltpu.VMEM((1, cols), f32),
        grad=pltpu.VMEM((block, cols), bf16),
        rank_out=each(lambda size: (N, size, width)),
        rank_in=each(lambda size: (N, size, width)),
        ranks=each(lambda size: (N, size, width)),
        cross_buf=pltpu.VMEM((block, cols), bf16),
        grad_out=each(lambda size: (slots, size, emb)),
        grad_pass=each(lambda size: (2, Y * size, emb)),
        grad_in=each(lambda size: (2, Y * size, emb)),
        row_out=pltpu.VMEM((N, rows_dev, emb), bf16),
        row_in=pltpu.VMEM((N, rows_dev, emb), bf16),
        load_sem=dma((Z + 4,)), store_sem=dma((n_parts,)), send_sem=dma((96,)),
        count_sem=dma((n_parts, 2)), row_sem=dma, column_sem=dma((3,)), rank_block_sem=dma((2, 2)),
        dense_sem=dma((n_parts,)), rank_sem=dma((n_parts,)), ranks_sem=dma((n_parts,)),
        back_sem=dma((n_parts, 2)), grad_sem=dma((n_parts, 2)), part_sem=dma, sibling_sem=dma,
    )
    names = (
        "rows_ref", "counts_ref", "state_ref", "down_ref", "up_ref", "bias_ref", "grad_ref",
        "crossed_ref", "new_ref", *scratch)
    return pl.pallas_call(
        functools.partial(kernel, n_wide, N, names),
        out_shape=(
            jax.ShapeDtypeStruct((block, cols), bf16),
            jax.ShapeDtypeStruct((1, rows_dev, emb), f32),
        ),
        in_specs=[vmem, hbm, vmem, hbm, hbm, hbm, hbm],
        out_specs=(hbm, vmem),
        scratch_shapes=tuple(scratch.values()),
        compiler_params=pltpu.CompilerParams(
            collective_id=0, has_side_effects=True, vmem_limit_bytes=60 * 1024 * 1024
        ),
    )(
        gathered_rows, bag_counts, row_state, cross_down.reshape(Y, RANK_ROWS, -1),
        cross_up.reshape(Y, RANK_ROWS, -1), cross_bias.reshape(1, -1), upstream,
    )


def solution(mesh):
    placed = (
        P("wide", "narrow", None),
        P("wide", "narrow", None),
        P("wide", "narrow"),
        P("narrow", None),
        P("narrow", None),
        P(),
        P("wide", "narrow"),
    )
    return jax.shard_map(
        on_device,
        mesh=mesh,
        in_specs=placed,
        out_specs=(P("wide", "narrow"), P("wide", "narrow", None)),
        check_vma=False,
    )
```

```python
import functools
import types
import jax
import jax.numpy as jnp
from jax import lax
from jax.experimental import pallas as pl
from jax.experimental.pallas import tpu as pltpu
from jax.sharding import PartitionSpec as P

learning_rate = 0.2
Y = 4
RANK_ROWS = 16
MESH = pl.DeviceIdType.MESH


def split(block):
    most = -(-block // 96) * 32
    return tuple(min(most, block - first) for first in range(0, block, most))


def kernel(n_wide, n_narrow, names, *refs):
    m = types.SimpleNamespace(**dict(zip(names, refs, strict=True)))
    f32, bf16 = jnp.float32, jnp.bfloat16
    Z, N = n_wide // Y, n_narrow
    half, quarter = Z // 2, Z // 4
    block, cols = m.grad_ref.shape
    rows_dev, emb = m.rows_ref.shape[1:]
    slots = cols // emb
    unit, quad = Y * block, cols // Y
    per_quad = quad // emb
    ranks_all = Y * N * RANK_ROWS
    sizes = split(block)
    starts = [sum(sizes[:h]) for h in range(len(sizes))]
    parts = range(len(sizes))
    w, n = lax.axis_index("wide"), lax.axis_index("narrow")
    z, y = w // Y, w % Y
    zq = z % Y

    def shift(k, j):
        x, c = k // 2, k % 2
        if j == 0:
            return jnp.where(c == 0, half - x, jnp.where(x == 0, Z - quarter, half + x))
        return jnp.where(
            c == 0, jnp.where(x == 0, quarter, x), jnp.where(x == 0, 0, Z - x))

    def unshift(d):
        e = jnp.where(d > half, Z - d, d)
        x = jnp.where(e == quarter, 0, jnp.where(e < quarter, e, half - e))
        c = jnp.where((d == 0) | (d > half), 1, 0)
        j = jnp.where((e > quarter) | (d == Z - quarter), 0, 1)
        return 2 * x + c, j

    pending = []
    used = [0]

    def new_send():
        used[0] += 1
        return m.send_sem.at[used[0] - 1]

    def wait_bytes(ref, sem):
        pltpu.make_async_copy(ref, ref, sem).wait()

    def later(ref, sem):
        pending.append(lambda: wait_bytes(ref, sem))

    def remote(src, dst, send, sem, to):
        return pltpu.make_async_remote_copy(
            src_ref=src, dst_ref=dst, send_sem=send, recv_sem=sem,
            device_id=to, device_id_type=MESH,
        )

    def move(src, dst, sem, here, to):
        send = new_send()

        @pl.when(jnp.logical_not(here))
        def _():
            remote(src, dst, send, sem, to).start()

        @pl.when(here)
        def _():
            pltpu.make_async_copy(src, dst, sem).start()

        def wait():
            @pl.when(jnp.logical_not(here))
            def _():
                wait_bytes(src, send)

        pending.append(wait)

    def finish():
        for wait in pending:
            wait()
        pending.clear()

    barrier = pltpu.get_barrier_semaphore()

    @pl.loop(1, Y * N)
    def _(i):
        to = (y * N + n + i) % (Y * N)
        pl.semaphore_signal(barrier, inc=1, device_id=(z * Y + to // N, to % N), device_id_type=MESH)

    for step in (1, 2, Z - 2, Z - 1):
        pl.semaphore_signal(barrier, inc=1, device_id=((z + step) % Z * Y + y, n), device_id_type=MESH)

    for j in range(2):
        @pl.when(shift(n, j) != 0)
        def _():
            to = (z + shift(n, j)) % Z * Y + y
            pl.semaphore_signal(barrier, inc=1, device_id=(to, n), device_id_type=MESH)

    @pl.loop(0, slots)
    def _(i):
        zt, yt = 2 * n + i // Y, i % Y
        k, _ = unshift((z + Z - zt) % Z)

        @pl.when(jnp.logical_not((zt == z) & (yt == y) & (k == n)))
        def _():
            pl.semaphore_signal(barrier, inc=1, device_id=(zt * Y + yt, k), device_id_type=MESH)

    pools_for_itself = jnp.where((shift(n, 1) == 0) & (z // 2 == n), 1, 0)

    def load_unit(i, j):
        u = (z + shift((n + 1 + i) % N, j)) % Z
        pltpu.make_async_copy(
            m.counts_ref.at[0, :, pl.ds(pl.multiple_of(u * unit, unit), unit)],
            m.raw.at[u], m.load_sem.at[u],
        ).start()

    def chip_blocks(k):
        for which, ref in enumerate((m.down_ref, m.up_ref)):
            for q in range(Y):
                yield (
                    ref.at[:, :, pl.ds(pl.multiple_of(k * cols + q * quad, quad), quad)],
                    m.weights.at[which, q, :, n])

    pl.loop(0, N)(functools.partial(load_unit, j=0))
    fixed = [pltpu.make_async_copy(a, b, m.load_sem.at[Z + 2]) for a, b in chip_blocks(n)]
    own_blocks = m.weights.at[:, :, :, 0]

    def load_shares(k):
        def load(ref, q, into):
            first = pl.multiple_of(k * cols + q * quad, quad)
            pltpu.make_async_copy(
                ref.at[y, :, pl.ds(first, quad)], into, m.load_sem.at[Z + 3]).start()

        for q in range(Y):
            load(m.down_ref, q, m.down_share.at[k, q])
        load(m.up_ref, zq, m.up_share.at[k])

    small = [
        pltpu.make_async_copy(
            m.bias_ref.at[:, pl.ds(pl.multiple_of(n * cols, cols), cols)],
            m.bias, m.load_sem.at[Z]),
        pltpu.make_async_copy(m.grad_ref, m.grad, m.load_sem.at[Z + 1]),
    ]
    pl.loop(0, N)(load_shares)
    pl.loop(0, N)(functools.partial(load_unit, j=1))
    for copy in small + fixed:
        copy.start()

    def code_unit(i, j):
        u = (z + shift((n + 1 + i) % N, j)) % Z
        wait_bytes(m.raw.at[u], m.load_sem.at[u])
        values = m.raw[u].astype(f32)
        for h in parts:
            lanes = [
                values[:, a * block + starts[h]:a * block + starts[h] + sizes[h]] for a in range(Y)]
            m.coded[h][u] = jnp.concatenate(lanes, axis=1).astype(bf16)

    pl.loop(0, N)(functools.partial(code_unit, j=0))
    m.rows_all[n] = m.rows_ref[0]
    wait_bytes(m.down_share, m.load_sem.at[Z + 3])
    wait_bytes(m.up_share, m.load_sem.at[Z + 3])
    pl.semaphore_wait(
        barrier, Y * N + 5 + slots - pools_for_itself - jnp.where(shift(n, 1) == 0, 1, 0))

    sends = [new_send() for _ in range(4)]

    @pl.loop(2, N)
    def _(i):
        k = (n // 2 * 2 + i) % N
        remote(
            m.down_share.at[k], m.weights.at[0, :, y, n], sends[1], m.column_sem.at[0], (w, k)
        ).start()

    @pl.loop(2, N)
    def _(i):
        k = (n // 2 * 2 + i) % N
        remote(
            m.up_share.at[k], m.weights.at[1, zq, y, n], sends[3], m.column_sem.at[2], (w, k)
        ).start()

    @pl.loop(1, N)
    def _(i):
        remote(m.rows_ref.at[0], m.rows_all.at[n], sends[0], m.row_sem, (w, (n + i) % N)).start()

    later(m.rows_all.at[pl.ds(0, N - 1)], sends[0])
    later(m.weights.at[0, :, 0, pl.ds(0, N - 2)], sends[1])
    later(m.weights.at[1, 0, 0, pl.ds(0, N - 2)], sends[3])

    def to_sibling():
        sibling = (w, n + 1 - 2 * (n % 2))
        for a, b in chip_blocks(sibling[1]):
            remote(a, b, sends[2], m.sibling_sem, sibling).start()
        later(own_blocks, sends[2])

    others = [(n // 2 + i) % (N // 2) * 2 for i in range(1, N // 2)]

    def spread_columns():
        wait_bytes(m.weights.at[1, 0, 0, pl.ds(0, N - 2)], m.column_sem.at[2])
        send = new_send()
        for step in (1, Z - 1, 2, Z - 2):
            for k in others:
                part = m.weights.at[1, zq, y, pl.ds(k, 2)]
                if step in (2, Z - 2):
                    part = m.weights.at[1, zq, y, k + (0 if step == 2 else 1)]
                remote(part, part, send, m.column_sem.at[1], ((z + step) % Z * Y + y, n)).start()
        later(m.weights.at[1, pl.ds(0, Y - 1), 0, pl.ds(0, N - 2)], send)

    def spread_ranks(which):
        if which == 0:
            wait_bytes(m.weights.at[0, :, 0, pl.ds(0, N - 2)], m.column_sem.at[0])
        else:
            wait_bytes(m.weights.at[1, pl.ds(0, Y - 1), 0, pl.ds(0, N - 2)], m.column_sem.at[1])
        send = new_send()
        for step in (1, Y - 1):
            for k in others:
                part = m.weights.at[which, :, y, pl.ds(k, 2)]
                remote(
                    part, part, send, m.rank_block_sem.at[which, 0], (z * Y + (y + step) % Y, n)
                ).start()
        later(m.weights.at[which, :, pl.ds(0, 2), pl.ds(0, N - 2)], send)

    def forward_ranks(which):
        wait_bytes(m.weights.at[which, :, pl.ds(0, 2), pl.ds(0, N - 2)], m.rank_block_sem.at[which, 0])
        send = new_send()
        for step, start in ((1, 0), (Y - 1, Y // 2)):
            for k in others:
                part = m.weights.at[which, pl.ds(start, Y // 2), (y + Y - step) % Y, pl.ds(k, 2)]
                remote(
                    part, part, send, m.rank_block_sem.at[which, 1], (z * Y + (y + step) % Y, n)
                ).start()
        later(m.weights.at[which, :, 0, pl.ds(0, N - 2)], send)

    def weights_here(which):
        wait_bytes(m.weights.at[which, :, 0, pl.ds(0, N - 2)], m.rank_block_sem.at[which, 1])

    def small_here():
        wait_bytes(own_blocks, m.sibling_sem)
        for copy in small + fixed:
            copy.wait()

    def send_units(h, j):
        send = new_send()

        @pl.loop(1, N)
        def _(i):
            k = (n + i) % N
            u = (z + shift(k, j)) % Z
            remote(m.coded[h].at[u], m.ct[h].at[j, n], send, m.count_sem.at[h, j], (w, k)).start()

        later(m.ct[h].at[j, pl.ds(0, N - 1)], send)

    send_units(0, 0)
    pl.loop(0, N)(functools.partial(code_unit, j=1))
    send_units(0, 1)
    spread_ranks(0)
    spread_columns()
    for h in parts[1:]:
        send_units(h, 0)
        send_units(h, 1)
    to_sibling()
    for h in parts:
        for j in range(2):
            m.ct[h][j, n] = m.coded[h][(z + shift(n, j)) % Z]

    def pool(h, j):
        wait_bytes(m.ct[h].at[j, pl.ds(0, N - 1)], m.count_sem.at[h, j])
        counts = m.ct[h][j].reshape(N * rows_dev, Y * sizes[h])
        table_rows = m.rows_all[...].reshape(N * rows_dev, emb)
        m.pooled[h][j] = lax.dot_general(
            counts, table_rows, (((0,), (0,)), ((), ())), preferred_element_type=f32
        ).astype(bf16)
        far = shift(n, j)
        zw = (z + far) % Z
        size = sizes[h]
        for i in range(Y):
            yd = (y + i) % Y
            move(
                m.pooled[h].at[j, pl.ds(pl.multiple_of(yd * size, 16), size)],
                m.dense[h].at[z % 2 * Y + y], m.dense_sem.at[h],
                (yd == y) & (z // 2 == n) & (zw == z), (zw * Y + yd, z // 2))

    def to_ranks(h):
        wait_bytes(m.dense[h], m.dense_sem.at[h])
        rows = pl.ds(starts[h], sizes[h])
        width = ranks_all * 2 // N
        send = new_send()
        for which in range(2):
            if h == 0:
                weights_here(which)
            total = 0.0
            for q in range(Y):
                x = jnp.concatenate(
                    [m.dense[h][q * per_quad + s] for s in range(per_quad)], axis=1)
                if which == 1:
                    slope = m.grad[rows, q * quad:(q + 1) * quad].astype(f32)
                    x = (slope * x.astype(f32)).astype(bf16)
                total += lax.dot_general(
                    x, m.weights[which, q].reshape(ranks_all, quad), (((1,), (1,)), ((), ())),
                    preferred_element_type=f32)
            first = which * (N // 2)
            for r in range(N // 2):
                m.rank_out[h][first + r] = total[:, r * width:(r + 1) * width].astype(bf16)

            @pl.loop(0, N // 2)
            def _(i):
                k = first + (n + i) % (N // 2)

                @pl.when(k != n)
                def _():
                    remote(
                        m.rank_out[h].at[k], m.rank_in[h].at[n], send, m.rank_sem.at[h], (w, k)
                    ).start()

        later(m.rank_out[h].at[pl.ds(0, N - 1)], send)
        m.rank_in[h][n] = m.rank_out[h][n]

    def sum_ranks(h):
        wait_bytes(m.rank_in[h].at[pl.ds(0, N - 1)], m.rank_sem.at[h])
        m.ranks[h][n] = jnp.sum(m.rank_in[h][...].astype(f32), axis=0).astype(bf16)
        send = new_send()

        @pl.loop(1, N)
        def _(i):
            remote(
                m.ranks[h].at[n], m.ranks[h].at[n], send, m.ranks_sem.at[h], (w, (n + i) % N)
            ).start()

        later(m.ranks[h].at[pl.ds(0, N - 1)], send)

    def from_ranks(h):
        wait_bytes(m.ranks[h].at[pl.ds(0, N - 1)], m.ranks_sem.at[h])
        size = sizes[h]
        rows = pl.ds(starts[h], size)
        low = jnp.concatenate([m.ranks[h][r] for r in range(N // 2)], axis=1)
        rank_grad = jnp.concatenate([m.ranks[h][r] for r in range(N // 2, N)], axis=1)
        for q in range(Y):
            here = slice(q * quad, (q + 1) * quad)
            lifted = jnp.dot(
                low, m.weights[1, q].reshape(ranks_all, quad), preferred_element_type=f32) + m.bias[:, here]
            back = jnp.dot(
                rank_grad, m.weights[0, q].reshape(ranks_all, quad), preferred_element_type=f32)
            x = jnp.concatenate(
                [m.dense[h][q * per_quad + s] for s in range(per_quad)], axis=1).astype(f32)
            slope = (m.grad[rows, here].astype(f32) * (lifted + 1.0) + back).astype(bf16)
            m.cross_buf[rows, here] = (x * lifted + x).astype(bf16)
            for s in range(per_quad):
                slot = q * per_quad + s
                m.grad_out[h][slot] = slope[:, s * emb:(s + 1) * emb]
                k, j = unshift((z + Z - (2 * n + slot // Y)) % Z)
                yt = slot % Y
                move(
                    m.grad_out[h].at[slot],
                    m.grad_pass[h].at[j, pl.ds(pl.multiple_of(y * size, 16), size)],
                    m.back_sem.at[h, j], (yt == y) & (k == n), (z * Y + yt, k))
        store = pltpu.make_async_copy(m.cross_buf.at[rows], m.crossed_ref.at[rows], m.store_sem.at[h])
        store.start()
        pending.append(store.wait)

    def pass_back(h, j):
        wait_bytes(m.grad_pass[h].at[j], m.back_sem.at[h, j])
        far = shift(n, j)
        move(
            m.grad_pass[h].at[j], m.grad_in[h].at[j], m.grad_sem.at[h, j],
            far == 0, ((z + Z - far) % Z * Y + y, n))

    def row_part(h, j):
        wait_bytes(m.grad_in[h].at[j], m.grad_sem.at[h, j])
        return jnp.dot(
            m.ct[h][j].reshape(N * rows_dev, Y * sizes[h]), m.grad_in[h][j],
            preferred_element_type=f32)

    wait_bytes(m.rows_all.at[pl.ds(0, N - 1)], m.row_sem)
    spread_ranks(1)
    pool(0, 0)
    pool(0, 1)
    forward_ranks(0)
    pool(1, 0)
    forward_ranks(1)
    pool(1, 1)
    for h in parts[2:]:
        pool(h, 0)
        pool(h, 1)
    small_here()

    def step_back(h):
        pass_back(h, 0)
        pass_back(h, 1)

    to_ranks(0)
    for h in parts:
        sum_ranks(h)
        if h + 1 < len(sizes):
            to_ranks(h + 1)
        if h > 0:
            step_back(h - 1)
        from_ranks(h)
    step_back(parts[-1])
    part = 0.0
    for h in parts:
        part += row_part(h, 0) + row_part(h, 1)
    m.row_out[...] = part.astype(bf16).reshape(N, rows_dev, emb)
    last = new_send()

    @pl.loop(1, N)
    def _(i):
        k = (n + i) % N
        remote(m.row_out.at[k], m.row_in.at[n], last, m.part_sem, (w, k)).start()

    m.row_in[n] = m.row_out[n]
    square = (rows_dev, rows_dev)
    diagonal = lax.broadcasted_iota(jnp.int32, square, 0) == lax.broadcasted_iota(jnp.int32, square, 1)
    state = jnp.sum(jnp.where(diagonal, m.state_ref[...], 0.0), axis=1, keepdims=True)
    finish()
    wait_bytes(m.row_in.at[pl.ds(0, N - 1)], m.part_sem)
    row_grad = jnp.sum(m.row_in[...].astype(f32), axis=0)
    state = state + jnp.mean(row_grad * row_grad, axis=1, keepdims=True)
    m.new_ref[0] = m.rows_ref[0].astype(f32) - learning_rate * row_grad / jnp.sqrt(state)
    wait_bytes(m.row_out.at[pl.ds(0, N - 1)], last)


def on_device(gathered_rows, bag_counts, row_state, cross_down, cross_up, cross_bias, upstream):
    f32, bf16 = jnp.float32, jnp.bfloat16
    n_wide, N = lax.axis_size("wide"), lax.axis_size("narrow")
    Z = n_wide // Y
    rows_dev, emb = gathered_rows.shape[1:]
    block, cols = upstream.shape
    unit, slots = Y * block, cols // emb
    width = 2 * cross_down.shape[0]
    sizes = split(block)
    n_parts = len(sizes)
    vmem = pl.BlockSpec(memory_space=pltpu.VMEM)
    hbm = pl.BlockSpec(memory_space=pl.ANY)
    dma = pltpu.SemaphoreType.DMA

    def each(shape_of, dtype=bf16):
        return tuple(pltpu.VMEM(shape_of(size), dtype) for size in sizes)

    scratch = dict(
        raw=pltpu.VMEM((Z, rows_dev, unit), jnp.int32),
        coded=each(lambda size: (Z, rows_dev, Y * size)),
        ct=each(lambda size: (2, N, rows_dev, Y * size)),
        rows_all=pltpu.VMEM((N, rows_dev, emb), bf16),
        pooled=each(lambda size: (2, Y * size, emb)),
        dense=each(lambda size: (slots, size, emb)),
        weights=pltpu.VMEM((2, Y, Y, N, RANK_ROWS, cols // Y), bf16),
        down_share=pltpu.VMEM((N, Y, RANK_ROWS, cols // Y), bf16),
        up_share=pltpu.VMEM((N, RANK_ROWS, cols // Y), bf16),
        bias=pltpu.VMEM((1, cols), f32),
        grad=pltpu.VMEM((block, cols), bf16),
        rank_out=each(lambda size: (N, size, width)),
        rank_in=each(lambda size: (N, size, width)),
        ranks=each(lambda size: (N, size, width)),
        cross_buf=pltpu.VMEM((block, cols), bf16),
        grad_out=each(lambda size: (slots, size, emb)),
        grad_pass=each(lambda size: (2, Y * size, emb)),
        grad_in=each(lambda size: (2, Y * size, emb)),
        row_out=pltpu.VMEM((N, rows_dev, emb), bf16),
        row_in=pltpu.VMEM((N, rows_dev, emb), bf16),
        load_sem=dma((Z + 4,)), store_sem=dma((n_parts,)), send_sem=dma((96,)),
        count_sem=dma((n_parts, 2)), row_sem=dma, column_sem=dma((3,)), rank_block_sem=dma((2, 2)),
        dense_sem=dma((n_parts,)), rank_sem=dma((n_parts,)), ranks_sem=dma((n_parts,)),
        back_sem=dma((n_parts, 2)), grad_sem=dma((n_parts, 2)), part_sem=dma, sibling_sem=dma,
    )
    names = (
        "rows_ref", "counts_ref", "state_ref", "down_ref", "up_ref", "bias_ref", "grad_ref",
        "crossed_ref", "new_ref", *scratch)
    return pl.pallas_call(
        functools.partial(kernel, n_wide, N, names),
        out_shape=(
            jax.ShapeDtypeStruct((block, cols), bf16),
            jax.ShapeDtypeStruct((1, rows_dev, emb), f32),
        ),
        in_specs=[vmem, hbm, vmem, hbm, hbm, hbm, hbm],
        out_specs=(hbm, vmem),
        scratch_shapes=tuple(scratch.values()),
        compiler_params=pltpu.CompilerParams(
            collective_id=0, has_side_effects=True, vmem_limit_bytes=60 * 1024 * 1024
        ),
    )(
        gathered_rows, bag_counts, row_state, cross_down.reshape(Y, RANK_ROWS, -1),
        cross_up.reshape(Y, RANK_ROWS, -1), cross_bias.reshape(1, -1), upstream,
    )


def solution(mesh):
    placed = (
        P("wide", "narrow", None),
        P("wide", "narrow", None),
        P("wide", "narrow"),
        P("narrow", None),
        P("narrow", None),
        P(),
        P("wide", "narrow"),
    )
    return jax.shard_map(
        on_device,
        mesh=mesh,
        in_specs=placed,
        out_specs=(P("wide", "narrow"), P("wide", "narrow", None)),
        check_vma=False,
    )
```
